128 devices in a mesh: section: 4 (over x_hi, core), dp: 32 (over z, x_lo, y).
Axes of the slice: x: 4 (x_hi: 2, x_lo: 2; x = x_hi * 2 + x_lo), y: 4, z: 4, core: 2. Of those that a mesh axis runs over, the one named last changes fastest.
Arguments:
- factor_rows: bfloat16 [1, 4, 6144, 3072], P(None, 'section', 'dp'), may hold values from -50.4 to 50.4
- entry_rows: bfloat16 [1, 6144, 3072], P(None, 'dp'), may hold values from -50.4 to 50.4
Outputs:
- diagonal_blocks: bfloat16 [1, 4, 3072, 3072], P(None, 'section', 'dp')
- adjacent_blocks: bfloat16 [1, 4, 3072, 3072], P(None, 'section', 'dp')
The draws below stay inside these ranges and needn't reach their ends.
All inputs are finite; a program needn't handle non-finite values.
Results may differ from the reference program's by a relative error of at most 0.001.
Values may be sent and summed in bfloat16 or wider, within the bound.
A program may use at most 128 MiB of HBM per device.

```python
import math
import jax
import jax.numpy as jnp

D = 3072
FACTORS = 1
TOKENS = 6144
LAYERS = 4


scale_floor = math.log(0.3)


scale_ceiling = math.log(3.0)


def common_parts(key):
    first_key, second_key, third_key = jax.random.split(key, 3)
    token_scale = jnp.exp(jax.random.uniform(first_key, (FACTORS, TOKENS, 1), jnp.float32, scale_floor, scale_ceiling))
    feature_scale = jnp.exp(jax.random.uniform(second_key, (FACTORS, 1, D), jnp.float32, scale_floor, scale_ceiling))
    normal_base = jnp.clip(jax.random.normal(third_key, (FACTORS, TOKENS, D), jnp.float32), -4.0, 4.0)
    return (normal_base, token_scale * feature_scale)


def draw_factor_rows(key, part):
    normal_base, scales = common_parts(key)
    key = jax.random.fold_in(key, 11)
    normal_key = jax.random.fold_in(key, 0)
    shape = (FACTORS, LAYERS, TOKENS, D)
    base = normal_base
    innovation = jnp.clip(jax.random.normal(normal_key, shape, jnp.float32), -4.0, 4.0)
    rows = (0.8 * base[:, None] + 0.6 * innovation) * scales[:, None]
    return rows.astype(jnp.bfloat16)


def draw_entry_rows(key, part):
    normal_base, scales = common_parts(key)
    key = jax.random.fold_in(key, 12)
    normal_key = jax.random.fold_in(key, 0)
    shape = (FACTORS, TOKENS, D)
    base = normal_base
    innovation = jnp.clip(jax.random.normal(normal_key, shape, jnp.float32), -4.0, 4.0)
    rows = (0.8 * base + 0.6 * innovation) * scales
    return rows.astype(jnp.bfloat16)


def setup_inputs(seed: int = 0) -> dict:
    key_list = jax.random.split(jax.random.key(seed), 3)
    factor_rows = draw_factor_rows(jax.random.fold_in(key_list[2], 71), 0)
    entry_rows = draw_entry_rows(jax.random.fold_in(key_list[2], 71), 0)
    return dict(factor_rows=factor_rows, entry_rows=entry_rows)


def reference(factor_rows, entry_rows):
    inverse = 1.0 / TOKENS
    diagonal_list = []
    adjacent_list = []
    for factor in range(FACTORS):
        previous = entry_rows[factor]
        square_row = []
        crossed_row = []
        for layer_index in range(LAYERS):
            current = factor_rows[factor, layer_index]
            square = jnp.dot(current.T, current, preferred_element_type=jnp.float32) * inverse
            crossed = jnp.dot(previous.T, current, preferred_element_type=jnp.float32) * inverse
            square_row.append(square.astype(jnp.bfloat16))
            crossed_row.append(crossed.astype(jnp.bfloat16))
            previous = current
        diagonal_list.append(jnp.stack(square_row))
        adjacent_list.append(jnp.stack(crossed_row))
    return (jnp.stack(diagonal_list), jnp.stack(adjacent_list))
```

```python
import functools

import jax
import jax.numpy as jnp
from jax import lax
from jax.experimental import pallas as pl
from jax.experimental.pallas import tpu as pltpu
from jax.sharding import PartitionSpec as P

MESH = pl.DeviceIdType.MESH
RING = 4
ROWS = 192
BLOCK = 768
HALF = 384
SUB = 256
SUBS = BLOCK // SUB
OWNED = 96
PIECES = (0, 1, 3, 2)
FORWARD = ((-1, 0), (1, 3), (-1, 1), (1, 2))


def device(x_hi, x_lo, y, z, core):
    return (x_hi * 2 + core, z * 8 + x_lo * 4 + y)


def turn(position, by):
    return lax.rem(position + by + RING, RING)


def kernel(
    inverse, x_ref, e_ref, d_ref, a_ref, left, right, prev, sent, got, kept, rounded,
    left_send, left_recv, right_send, right_recv, prev_send, prev_recv, pass_send, local_sem,
    x_send, x_recv, out_send, out_recv,
):
    section = lax.axis_index("section")
    group = lax.axis_index("dp")
    x_hi, core = section // 2, lax.rem(section, 2)
    z, x_lo, y = group // 8, lax.rem(group // 4, 2), lax.rem(group, 4)
    here = functools.partial(device, x_hi, x_lo)
    x_partner = device(x_hi, 1 - x_lo, y, z, core)
    other_core = device(x_hi, x_lo, y, z, 1 - core)

    barrier = pltpu.get_barrier_semaphore()

    def greet(target):
        pl.semaphore_signal(barrier, inc=1, device_id=target, device_id_type=MESH)

    for step in range(1, RING):
        greet(here(turn(y, step), z, core))
        greet(here(y, turn(z, step), core))
    greet(x_partner)
    greet(other_core)
    expected = 8

    @pl.when(core == 0)
    def _():
        for step in range(RING):
            @pl.when((z != y) | (step != 0))
            def _():
                greet(here(z, turn(z, step), core))

        @pl.when(x_hi == 1)
        def _():
            for row in range(RING):
                greet(device(0, x_lo, row, z, 1))

    expected = expected + jnp.where(
        core == 0, jnp.where(z == y, 3, 4), jnp.where(x_hi == 0, 4, 0)
    )
    pl.semaphore_wait(barrier, expected)

    def remote(src, dst, send, recv, target):
        return pltpu.make_async_remote_copy(
            src_ref=src, dst_ref=dst, send_sem=send, recv_sem=recv, device_id=target, device_id_type=MESH
        )

    def slot(row_z, row_y):
        return row_z * RING + row_y

    def piece(buffer, index):
        return buffer.at[pl.ds(pl.multiple_of(index * ROWS, ROWS), ROWS)]

    def columns(ref, index):
        return ref.at[:, pl.ds(pl.multiple_of(index * BLOCK, BLOCK), BLOCK)]

    mine = slot(z, y)

    class Flow:
        def __init__(self, buffer, send, recv, along_z):
            self.buffer, self.send, self.recv, self.along_z = buffer, send, recv, along_z
            self.count = 0
            self.copies = []

        def start(self, src, index, target):
            copy = remote(src, piece(self.buffer, index), self.send.at[self.count], self.recv.at[index], target)
            copy.start()
            self.count += 1
            self.copies.append(copy)

        def wait(self, index):
            whole = piece(self.buffer, index)
            remote(whole, whole, self.send.at[0], self.recv.at[index], x_partner).wait_recv()

        def spread(self, src):
            for step in (1, 3, 2):
                if self.along_z:
                    to = turn(y, step)
                    target = here(to, z, core)
                else:
                    to = turn(z, step)
                    target = here(y, to, core)
                self.start(columns(src, to), mine, target)

        def keep(self, src, sem):
            own = y if self.along_z else z
            copy = pltpu.make_async_copy(columns(src, own), piece(self.buffer, mine), self.recv.at[mine])
            copy.start()

        def index(self, step, part):
            if self.along_z:
                return slot(turn(z, step), turn(y, part))
            return slot(turn(z, part), turn(y, step))

        def neighbour(self, step):
            return here(y, turn(z, step), core) if self.along_z else here(turn(y, step), z, core)

        def push(self, index, step):
            self.start(piece(self.buffer, index), index, self.neighbour(step))

        def own(self, part):
            index = self.index(0, part)
            self.wait(index)
            self.push(index, 1)
            self.push(index, -1)
            return index

        def relay(self, step, part):
            index = self.index(step, part)
            self.wait(index)
            self.push(index, -step)
            return index

        def rest(self):
            return [self.index(s, p) for s, ps in ((-1, (3, 2)), (1, (0, 1)), (2, PIECES)) for p in ps]

    def product(lhs, rhs, half, sub):
        start = pl.multiple_of(half * HALF, HALF)
        return lax.dot_general(
            lhs[:, pl.ds(start, HALF)],
            rhs[:, pl.ds(pl.multiple_of(sub * SUB, SUB), SUB)],
            (((0,), (0,)), ((), ())),
            preferred_element_type=jnp.float32,
        )

    def x_copy(which, sub):
        return remote(
            sent.at[which, sub], got.at[which, sub], x_send.at[which, sub], x_recv.at[which, sub], x_partner
        )

    def partner_half(which, lhs, rhs):
        @pl.loop(0, SUBS)
        def _(sub):
            sent[which, sub] = product(lhs, rhs, 1 - x_lo, sub)
            x_copy(which, sub).start()

    def own_half(which, lhs, rhs):
        @pl.loop(0, SUBS)
        def _(sub):
            kept[which, sub] = product(lhs, rhs, x_lo, sub)

    def out_copy(which, out, turned, sub, owner, start):
        block, row_z = (z, y) if turned else (y, z)
        src = rounded.at[which, sub, pl.ds(owner * OWNED, OWNED)]
        dst = out.at[:, pl.ds(pl.multiple_of(block * BLOCK + sub * SUB, SUB), SUB)]
        recv = out_recv.at[which, block, sub]
        itself = (owner == y) & (row_z == z)

        @pl.when(itself)
        def _():
            if start:
                pltpu.make_async_copy(src, dst, recv).start()

        @pl.when(jnp.logical_not(itself))
        def _():
            copy = remote(src, dst, out_send.at[which, sub, owner], recv, here(owner, row_z, core))
            if start:
                copy.start()
            else:
                copy.wait_send()

    def finish(which, out, turned):
        @pl.loop(0, SUBS)
        def _(sub):
            x_copy(which, sub).wait_recv()
            rounded[which, sub] = ((kept[which, sub] + got[which, sub]) * inverse).astype(jnp.bfloat16)
            for owner in range(RING):
                out_copy(which, out, turned, sub, owner, True)

    def drain(which, out, turned):
        @pl.loop(0, SUBS)
        def _(sub):
            x_copy(which, sub).wait_send()
            for owner in range(RING):
                out_copy(which, out, turned, sub, owner, False)
            for block in range(RING):
                dst = out.at[:, pl.ds(pl.multiple_of(block * BLOCK + sub * SUB, SUB), SUB)]
                remote(
                    rounded.at[which, sub, pl.ds(0, OWNED)], dst, out_send.at[which, sub, 0],
                    out_recv.at[which, block, sub], x_partner,
                ).wait_recv()

    @pl.when(core == 0)
    def _():
        lefts = Flow(left, left_send, left_recv, False)
        rights = Flow(right, right_send, right_recv, True)
        prevs = Flow(prev, prev_send, prev_recv, True)
        passed = []

        def hand_over(index):
            copy = remote(piece(left, index), piece(prev, index), pass_send.at[len(passed)], prev_recv.at[index], other_core)
            copy.start()
            passed.append(copy)

        lefts.keep(x_ref, local_sem)
        rights.keep(x_ref, local_sem)
        lefts.spread(x_ref)
        rights.spread(x_ref)
        for part in PIECES:
            hand_over(lefts.own(part))
            rights.own(part)

        @pl.when(x_hi == 0)
        def _():
            prevs.keep(e_ref, local_sem)
            prevs.spread(e_ref)
        first = list(prevs.copies)
        prevs.copies = []

        for step, part in FORWARD:
            hand_over(lefts.relay(step, part))
            rights.relay(step, part)
        for part in PIECES:
            prevs.own(part)
        for index in lefts.rest():
            lefts.wait(index)
            hand_over(index)
        for index in rights.rest():
            rights.wait(index)
        partner_half(0, left, right)
        for step, part in FORWARD[:2]:
            prevs.relay(step, part)
        own_half(0, left, right)
        for step, part in FORWARD[2:]:
            prevs.relay(step, part)
        finish(0, d_ref, False)
        for index in prevs.rest():
            prevs.wait(index)
        partner_half(1, prev, left)
        own_half(1, prev, left)
        finish(1, a_ref, True)
        drain(0, d_ref, False)
        drain(1, a_ref, True)
        for copy in lefts.copies + rights.copies + prevs.copies + passed:
            copy.wait_send()

        @pl.when(x_hi == 0)
        def _():
            for count, _ in enumerate(first):
                remote(piece(prev, mine), piece(prev, mine), prev_send.at[count], prev_recv.at[mine], x_partner).wait_send()

    @pl.when(core == 1)
    def _():
        lefts = Flow(left, left_send, left_recv, False)
        rights = Flow(right, right_send, right_recv, True)
        prevs = Flow(prev, prev_send, prev_recv, False)
        lefts.keep(x_ref, local_sem)
        rights.keep(x_ref, local_sem)
        lefts.spread(x_ref)
        rights.spread(x_ref)

        def relayed(to):
            return remote(
                columns(x_ref, to), piece(prev, mine), prev_send.at[to], prev_recv.at[mine], device(1, x_lo, to, z, 0)
            )

        @pl.when(x_hi == 0)
        def _():
            for to in range(RING):
                relayed(to).start()

        for part in PIECES:
            prevs.wait(prevs.index(0, part))
        for part in PIECES:
            lefts.own(part)
            rights.own(part)
        for step, part in FORWARD:
            lefts.relay(step, part)
            rights.relay(step, part)
        for step, part in FORWARD:
            prevs.wait(prevs.index(step, part))
        for index in prevs.rest():
            prevs.wait(index)
        for index in rights.rest():
            rights.wait(index)
        partner_half(1, prev, right)
        own_half(1, prev, right)
        for index in lefts.rest():
            lefts.wait(index)
        partner_half(0, left, right)
        own_half(0, left, right)
        finish(1, a_ref, False)
        finish(0, d_ref, False)
        drain(1, a_ref, False)
        drain(0, d_ref, False)
        for copy in lefts.copies + rights.copies:
            copy.wait_send()

        @pl.when(x_hi == 0)
        def _():
            for to in range(RING):
                relayed(to).wait_send()


def on_device(factor_rows, entry_rows):
    rows, width = factor_rows.shape[2:]
    tokens = rows * lax.axis_size("dp")
    out = jax.ShapeDtypeStruct((OWNED, width), jnp.bfloat16)
    block = pltpu.VMEM((tokens // 2, BLOCK), jnp.bfloat16)
    part = pltpu.VMEM((2, SUBS, HALF, SUB), jnp.float32)
    slots = pltpu.SemaphoreType.DMA((16,))
    diagonal, adjacent = pl.pallas_call(
        functools.partial(kernel, 1.0 / tokens),
        out_shape=(out, out),
        in_specs=[pl.BlockSpec(memory_space=pl.ANY)] * 2,
        out_specs=[pl.BlockSpec(memory_space=pl.ANY)] * 2,
        scratch_shapes=[block, block, block, part, part, part, pltpu.VMEM((2, SUBS, HALF, SUB), jnp.bfloat16)]
        + [slots] * 7
        + [
            pltpu.SemaphoreType.DMA,
            pltpu.SemaphoreType.DMA((2, SUBS)),
            pltpu.SemaphoreType.DMA((2, SUBS)),
            pltpu.SemaphoreType.DMA((2, SUBS, RING)),
            pltpu.SemaphoreType.DMA((2, RING, SUBS)),
        ],
        compiler_params=pltpu.CompilerParams(
            collective_id=0, has_side_effects=True, vmem_limit_bytes=60 * 2**20
        ),
        cost_estimate=pl.CostEstimate(flops=4 * BLOCK * BLOCK * tokens // 2, bytes_accessed=2**22, transcendentals=0),
        name="blocks",
    )(factor_rows.reshape(rows, width), entry_rows.reshape(rows, width))
    return diagonal.reshape(1, 1, OWNED, width), adjacent.reshape(1, 1, OWNED, width)


def solution(mesh):
    placed = (P(None, "section", "dp", None), P(None, "dp", None))
    return jax.shard_map(
        on_device,
        mesh=mesh,
        in_specs=placed,
        out_specs=(P(None, "section", "dp", None), P(None, "section", "dp", None)),
        check_vma=False,
    )
```

```python
import functools

import jax
import jax.numpy as jnp
from jax import lax
from jax.experimental import pallas as pl
from jax.experimental.pallas import tpu as pltpu
from jax.sharding import PartitionSpec as P

MESH = pl.DeviceIdType.MESH
RING = 4
ROWS = 192
BLOCK = 768
HALF = 384
OWNED = 96
DEPTH = 3
PIECES = (0, 1, 3, 2)
FORWARD = ((-1, 0), (1, 3), (-1, 1), (1, 2))


def device(x_hi, x_lo, y, z, core):
    return (x_hi * 2 + core, z * 8 + x_lo * 4 + y)


def turn(position, by):
    return lax.rem(position + by + RING, RING)


def remote(src, dst, send, recv, target):
    return pltpu.make_async_remote_copy(
        src_ref=src, dst_ref=dst, send_sem=send, recv_sem=recv, device_id=target, device_id_type=MESH
    )


def slot(row_z, row_y):
    return row_z * RING + row_y


class Flow:
    def __init__(self, place, buffer, send, recv, along_z, halves):
        self.here, self.y, self.z = place
        self.buffer, self.send, self.recv, self.along_z, self.halves = buffer, send, recv, along_z, halves
        self.copies = ([], [])
        self.flying = {1: [], -1: []}
        self.mine = slot(self.z, self.y)

    def piece(self, order, index):
        return self.buffer.at[self.halves[order], pl.ds(pl.multiple_of(index * ROWS, ROWS), ROWS)]

    def columns(self, src, order, block):
        start = pl.multiple_of(block * BLOCK + self.halves[order] * HALF, HALF)
        return src.at[:, pl.ds(start, HALF)]

    def start(self, src, order, index, target):
        half = self.halves[order]
        count = len(self.copies[order])
        copy = remote(src, self.piece(order, index), self.send.at[half, count], self.recv.at[half, index], target)
        copy.start()
        self.copies[order].append(copy)

    def wait(self, order, index):
        whole = self.piece(order, index)
        half = self.halves[order]
        remote(whole, whole, self.send.at[half, 0], self.recv.at[half, index], self.neighbour(1)).wait_recv()

    def spread(self, src, order):
        own = self.y if self.along_z else self.z
        pltpu.make_async_copy(
            self.columns(src, order, own), self.piece(order, self.mine), self.recv.at[self.halves[order], self.mine]
        ).start()
        for step in (1, 3, 2):
            to = turn(own, step)
            target = self.here(to, self.z) if self.along_z else self.here(self.y, to)
            self.start(self.columns(src, order, to), order, self.mine, target)

    def index(self, step, part):
        if self.along_z:
            return slot(turn(self.z, step), turn(self.y, part))
        return slot(turn(self.z, part), turn(self.y, step))

    def neighbour(self, step):
        return self.here(self.y, turn(self.z, step)) if self.along_z else self.here(turn(self.y, step), self.z)

    def push(self, order, index, step):
        flying = self.flying[step]
        if len(flying) == DEPTH:
            past, count = flying.pop(0)
            self.copies[past][count].wait_send()
            self.copies[past][count] = None
        flying.append((order, len(self.copies[order])))
        self.start(self.piece(order, index), order, index, self.neighbour(step))

    def own(self, order, part):
        index = self.index(0, part)
        self.wait(order, index)
        self.push(order, index, 1)
        self.push(order, index, -1)
        return index

    def relay(self, order, step, part):
        index = self.index(step, part)
        self.wait(order, index)
        self.push(order, index, -step)
        return index

    REST = ((-1, 3), (-1, 2), (1, 0), (1, 1), (2, 0), (2, 1), (2, 3), (2, 2))

    def rest(self):
        return [self.index(step, part) for step, part in self.REST]

    def wait_rest(self, order):
        for index in self.rest():
            self.wait(order, index)

    def drain(self, order, first=0):
        for copy in self.copies[order][first:]:
            if copy is not None:
                copy.wait_send()


def weave(relay, behind, own, ahead):
    relay(behind, *FORWARD[0])
    relay(behind, *FORWARD[1])
    own(ahead, 0)
    own(ahead, 1)
    relay(behind, *FORWARD[2])
    relay(behind, *FORWARD[3])
    own(ahead, 3)
    own(ahead, 2)


def kernel(
    inverse, x_ref, e_ref, d_ref, a_ref, left, right, prev, sent, got, kept, rounded,
    left_send, left_recv, right_send, right_recv, prev_send, prev_recv, pass_send,
    x_send, x_recv, out_send, out_recv,
):
    section = lax.axis_index("section")
    group = lax.axis_index("dp")
    x_hi, core = section // 2, lax.rem(section, 2)
    z, x_lo, y = group // 8, lax.rem(group // 4, 2), lax.rem(group, 4)

    def here(at_y, at_z):
        return device(x_hi, x_lo, at_y, at_z, core)

    place = (here, y, z)
    theirs, ours = 1 - x_lo, x_lo
    x_partner = device(x_hi, 1 - x_lo, y, z, core)
    other_core = device(x_hi, x_lo, y, z, 1 - core)

    barrier = pltpu.get_barrier_semaphore()

    def greet(target):
        pl.semaphore_signal(barrier, inc=1, device_id=target, device_id_type=MESH)

    for step in range(1, RING):
        greet(here(turn(y, step), z))
        greet(here(y, turn(z, step)))
    greet(x_partner)
    greet(other_core)

    @pl.when(core == 0)
    def _():
        for step in range(RING):
            @pl.when((z != y) | (step != 0))
            def _():
                greet(here(z, turn(z, step)))

        @pl.when(x_hi == 1)
        def _():
            for row in range(RING):
                greet(device(0, x_lo, row, z, 1))

    expected = 8 + jnp.where(core == 0, jnp.where(z == y, 3, 4), jnp.where(x_hi == 0, 4, 0))
    pl.semaphore_wait(barrier, expected)

    def product(lhs, rhs, row_half, column_half):
        return lax.dot_general(
            lhs[row_half], rhs[column_half], (((0,), (0,)), ((), ())), preferred_element_type=jnp.float32
        )

    def x_copy(which, half):
        return remote(
            sent.at[which, half], got.at[which, half], x_send.at[which, half], x_recv.at[which, half], x_partner
        )

    def partner_part(which, lhs, rhs, half):
        sent[which, half] = product(lhs, rhs, theirs, half)
        x_copy(which, half).start()

    def own_part(which, lhs, rhs, half):
        kept[which, half] = product(lhs, rhs, ours, half)

    def own_chunk(which, lhs, rhs, half, row_z, first):
        rows = pl.ds(pl.multiple_of(row_z * RING * ROWS, ROWS), RING * ROWS)
        value = lax.dot_general(
            lhs[ours, rows], rhs[half, rows], (((0,), (0,)), ((), ())), preferred_element_type=jnp.float32
        )
        kept[which, half] = value if first else kept[which, half] + value

    def out_copy(which, out, turned, half, owner, start):
        block, row_z = (z, y) if turned else (y, z)
        src = rounded.at[which, half, pl.ds(owner * OWNED, OWNED)]
        dst = out.at[:, pl.ds(pl.multiple_of(block * BLOCK + half * HALF, HALF), HALF)]
        recv = out_recv.at[which, block, half]
        itself = (owner == y) & (row_z == z)

        @pl.when(itself)
        def _():
            if start:
                pltpu.make_async_copy(src, dst, recv).start()

        @pl.when(jnp.logical_not(itself))
        def _():
            copy = remote(src, dst, out_send.at[which, half, owner], recv, here(owner, row_z))
            if start:
                copy.start()
            else:
                copy.wait_send()

    def finish(which, out, turned, half):
        x_copy(which, half).wait_recv()
        rounded[which, half] = ((kept[which, half] + got[which, half]) * inverse).astype(jnp.bfloat16)
        for owner in range(RING):
            out_copy(which, out, turned, half, owner, True)

    def drain(which, out, turned):
        @pl.loop(0, 2)
        def _(half):
            x_copy(which, half).wait_send()
            for owner in range(RING):
                out_copy(which, out, turned, half, owner, False)
            for block in range(RING):
                dst = out.at[:, pl.ds(pl.multiple_of(block * BLOCK + half * HALF, HALF), HALF)]
                remote(
                    rounded.at[which, half, pl.ds(0, OWNED)], dst, out_send.at[which, half, 0],
                    out_recv.at[which, block, half], x_partner,
                ).wait_recv()

    def relayed(half, to):
        return remote(
            x_ref.at[:, pl.ds(to * BLOCK + half * HALF, HALF)],
            prev.at[half, pl.ds(pl.multiple_of(slot(z, y) * ROWS, ROWS), ROWS)],
            prev_send.at[half, to], prev_recv.at[half, slot(z, y)], device(1, x_lo, to, z, 0),
        )

    @pl.when(core == 0)
    def _():
        lefts = Flow(place, left, left_send, left_recv, False, (theirs, ours))
        rights = Flow(place, right, right_send, right_recv, True, (0, 1))
        prevs = Flow(place, prev, prev_send, prev_recv, True, (theirs, ours))
        passed = []

        def hand_over(order, index):
            half = lefts.halves[order]
            whole = lefts.piece(order, index)
            to = prev.at[half, pl.ds(pl.multiple_of(index * ROWS, ROWS), ROWS)]
            copy = remote(whole, to, pass_send.at[half, index], prev_recv.at[half, index], other_core)
            copy.start()
            passed.append(copy)

        def rest_left(order):
            for index in lefts.rest():
                lefts.wait(order, index)
                hand_over(order, index)

        def left_own(order, part):
            hand_over(order, lefts.own(order, part))

        def left_relay(order, step, part):
            hand_over(order, lefts.relay(order, step, part))

        lefts.spread(x_ref, 0)
        for part in PIECES:
            left_own(0, part)
        lefts.spread(x_ref, 1)
        rights.spread(x_ref, 0)
        weave(left_relay, 0, left_own, 1)
        rights.spread(x_ref, 1)
        rest_left(0)
        weave(left_relay, 1, rights.own, 0)

        @pl.when(x_hi == 0)
        def _():
            for order in range(2):
                prevs.spread(e_ref, order)

        rest_left(1)
        weave(rights.relay, 0, rights.own, 1)
        rights.wait_rest(0)
        partner_part(0, left, right, 0)
        weave(rights.relay, 1, prevs.own, 0)
        rights.wait_rest(1)
        partner_part(0, left, right, 1)
        weave(prevs.relay, 0, prevs.own, 1)
        own_part(0, left, right, 0)
        prevs.wait_rest(0)
        partner_part(1, prev, left, 0)
        partner_part(1, prev, left, 1)
        for step, part in FORWARD:
            prevs.relay(1, step, part)
        own_part(0, left, right, 1)
        finish(0, d_ref, False, 0)
        for half in range(2):
            own_chunk(1, prev, left, half, z, True)
        finish(0, d_ref, False, 1)
        for step, part in prevs.REST[:4]:
            prevs.wait(1, prevs.index(step, part))
        for half in range(2):
            own_chunk(1, prev, left, half, turn(z, 1), False)
            own_chunk(1, prev, left, half, turn(z, -1), False)
        for step, part in prevs.REST[4:]:
            prevs.wait(1, prevs.index(step, part))
        for half in range(2):
            own_chunk(1, prev, left, half, turn(z, 2), False)
            finish(1, a_ref, True, half)
        drain(0, d_ref, False)
        drain(1, a_ref, True)
        for order in range(2):
            lefts.drain(order)
            rights.drain(order)
            prevs.drain(order, 3)
        for copy in passed:
            copy.wait_send()

        @pl.when(x_hi == 0)
        def _():
            for order in range(2):
                for count in range(3):
                    whole = prevs.piece(order, prevs.mine)
                    half = prevs.halves[order]
                    remote(whole, whole, prev_send.at[half, count], prev_recv.at[half, 0], x_partner).wait_send()

    @pl.when(core == 1)
    def _():
        lefts = Flow(place, left, left_send, left_recv, False, (theirs, ours))
        rights = Flow(place, right, right_send, right_recv, True, (0, 1))
        prevs = Flow(place, prev, prev_send, prev_recv, False, (theirs, ours))

        def wait_prev(order):
            for part in PIECES:
                prevs.wait(order, prevs.index(0, part))
            for step, part in FORWARD:
                prevs.wait(order, prevs.index(step, part))
            prevs.wait_rest(order)

        rights.spread(x_ref, 0)

        @pl.when(x_hi == 0)
        def _():
            for half in range(2):
                for to in range(RING):
                    relayed(half, to).start()

        for part in PIECES:
            rights.own(0, part)
        rights.spread(x_ref, 1)
        lefts.spread(x_ref, 0)
        weave(rights.relay, 0, rights.own, 1)
        lefts.spread(x_ref, 1)
        rights.wait_rest(0)
        wait_prev(0)
        partner_part(1, prev, right, 0)
        weave(rights.relay, 1, lefts.own, 0)
        rights.wait_rest(1)
        partner_part(1, prev, right, 1)
        weave(lefts.relay, 0, lefts.own, 1)
        lefts.wait_rest(0)
        partner_part(0, left, right, 0)
        partner_part(0, left, right, 1)
        for step, part in FORWARD:
            lefts.relay(1, step, part)
        wait_prev(1)
        own_part(1, prev, right, 0)
        finish(1, a_ref, False, 0)
        own_part(1, prev, right, 1)
        finish(1, a_ref, False, 1)
        lefts.wait_rest(1)
        own_part(0, left, right, 0)
        finish(0, d_ref, False, 0)
        own_part(0, left, right, 1)
        finish(0, d_ref, False, 1)
        drain(1, a_ref, False)
        drain(0, d_ref, False)
        for order in range(2):
            lefts.drain(order)
            rights.drain(order)

        @pl.when(x_hi == 0)
        def _():
            for half in range(2):
                for to in range(RING):
                    relayed(half, to).wait_send()


def on_device(factor_rows, entry_rows):
    rows, width = factor_rows.shape[2:]
    tokens = rows * lax.axis_size("dp")
    out = jax.ShapeDtypeStruct((OWNED, width), jnp.bfloat16)
    block = pltpu.VMEM((2, tokens // 2, HALF), jnp.bfloat16)
    part = pltpu.VMEM((2, 2, HALF, HALF), jnp.float32)
    slots = pltpu.SemaphoreType.DMA((2, 16))
    diagonal, adjacent = pl.pallas_call(
        functools.partial(kernel, 1.0 / tokens),
        out_shape=(out, out),
        in_specs=[pl.BlockSpec(memory_space=pl.ANY)] * 2,
        out_specs=[pl.BlockSpec(memory_space=pl.ANY)] * 2,
        scratch_shapes=[block, block, block, part, part, part, pltpu.VMEM((2, 2, HALF, HALF), jnp.bfloat16)]
        + [slots] * 7
        + [
            pltpu.SemaphoreType.DMA((2, 2)),
            pltpu.SemaphoreType.DMA((2, 2)),
            pltpu.SemaphoreType.DMA((2, 2, RING)),
            pltpu.SemaphoreType.DMA((2, RING, 2)),
        ],
        compiler_params=pltpu.CompilerParams(
            collective_id=0, has_side_effects=True, vmem_limit_bytes=60 * 2**20
        ),
        cost_estimate=pl.CostEstimate(flops=4 * BLOCK * BLOCK * tokens // 2, bytes_accessed=2**22, transcendentals=0),
        name="blocks",
    )(factor_rows.reshape(rows, width), entry_rows.reshape(rows, width))
    return diagonal.reshape(1, 1, OWNED, width), adjacent.reshape(1, 1, OWNED, width)


def solution(mesh):
    placed = (P(None, "section", "dp", None), P(None, "dp", None))
    return jax.shard_map(
        on_device,
        mesh=mesh,
        in_specs=placed,
        out_specs=(P(None, "section", "dp", None), P(None, "section", "dp", None)),
        check_vma=False,
    )
```

```python
import functools

import jax
import jax.numpy as jnp
from jax import lax
from jax.experimental import pallas as pl
from jax.experimental.pallas import tpu as pltpu
from jax.sharding import PartitionSpec as P

MESH = pl.DeviceIdType.MESH
RING = 4
ROWS = 192
BLOCK = 768
HALF = 384
OWNED = 96
DEPTH = 3
PIECES = (0, 1, 3, 2)
FORWARD = ((-1, 0), (1, 3), (-1, 1), (1, 2))


def device(x_hi, x_lo, y, z, core):
    return (x_hi * 2 + core, z * 8 + x_lo * 4 + y)


def turn(position, by):
    return lax.rem(position + by + RING, RING)


def remote(src, dst, send, recv, target):
    return pltpu.make_async_remote_copy(
        src_ref=src, dst_ref=dst, send_sem=send, recv_sem=recv, device_id=target, device_id_type=MESH
    )


def slot(row_z, row_y):
    return row_z * RING + row_y


class Flow:
    def __init__(self, place, buffer, send, recv, along_z, halves, kept=None):
        self.here, self.y, self.z = place
        self.buffer, self.send, self.recv, self.along_z, self.halves = buffer, send, recv, along_z, halves
        self.kept = halves if kept is None else kept
        self.copies = ([], [])
        self.flying = {1: [], -1: []}
        self.mine = slot(self.z, self.y)

    def piece(self, order, index):
        return self.buffer.at[self.kept[order], pl.ds(pl.multiple_of(index * ROWS, ROWS), ROWS)]

    def columns(self, src, order, block):
        start = pl.multiple_of(block * BLOCK + self.halves[order] * HALF, HALF)
        return src.at[:, pl.ds(start, HALF)]

    def start(self, src, order, index, target):
        half = self.kept[order]
        count = len(self.copies[order])
        copy = remote(src, self.piece(order, index), self.send.at[half, count], self.recv.at[half, index], target)
        copy.start()
        self.copies[order].append(copy)

    def wait(self, order, index):
        whole = self.piece(order, index)
        half = self.kept[order]
        remote(whole, whole, self.send.at[half, 0], self.recv.at[half, index], self.neighbour(1)).wait_recv()

    def spread(self, src, order):
        own = self.y if self.along_z else self.z
        pltpu.make_async_copy(
            self.columns(src, order, own), self.piece(order, self.mine), self.recv.at[self.kept[order], self.mine]
        ).start()
        for step in (1, 3, 2):
            to = turn(own, step)
            target = self.here(to, self.z) if self.along_z else self.here(self.y, to)
            self.start(self.columns(src, order, to), order, self.mine, target)

    def index(self, step, part):
        if self.along_z:
            return slot(turn(self.z, step), turn(self.y, part))
        return slot(turn(self.z, part), turn(self.y, step))

    def neighbour(self, step):
        return self.here(self.y, turn(self.z, step)) if self.along_z else self.here(turn(self.y, step), self.z)

    def push(self, order, index, step):
        flying = self.flying[step]
        if len(flying) == DEPTH:
            past, count = flying.pop(0)
            self.copies[past][count].wait_send()
            self.copies[past][count] = None
        flying.append((order, len(self.copies[order])))
        self.start(self.piece(order, index), order, index, self.neighbour(step))

    def own(self, order, part):
        index = self.index(0, part)
        self.wait(order, index)
        self.push(order, index, 1)
        self.push(order, index, -1)
        return index

    def relay(self, order, step, part):
        index = self.index(step, part)
        self.wait(order, index)
        self.push(order, index, -step)
        return index

    REST = ((-1, 3), (-1, 2), (1, 0), (1, 1), (2, 0), (2, 1), (2, 3), (2, 2))

    def rest(self):
        return [self.index(step, part) for step, part in self.REST]

    def wait_rest(self, order):
        for index in self.rest():
            self.wait(order, index)

    def drain(self, order, first=0):
        for copy in self.copies[order][first:]:
            if copy is not None:
                copy.wait_send()


def weave(relay, behind, own, ahead):
    relay(behind, *FORWARD[0])
    relay(behind, *FORWARD[1])
    own(ahead, 0)
    own(ahead, 1)
    relay(behind, *FORWARD[2])
    relay(behind, *FORWARD[3])
    own(ahead, 3)
    own(ahead, 2)


def kernel(
    inverse, x_ref, e_ref, d_ref, a_ref, left, right, prev, last, staged, sent, got, kept, rounded,
    left_send, left_recv, right_send, right_recv, prev_recv, last_send, last_recv, pass_send, relay_send, relay_recv,
    x_send, x_recv, out_send, out_recv,
):
    section = lax.axis_index("section")
    group = lax.axis_index("dp")
    x_hi, core = section // 2, lax.rem(section, 2)
    z, x_lo, y = group // 8, lax.rem(group // 4, 2), lax.rem(group, 4)

    def here(at_y, at_z):
        return device(x_hi, x_lo, at_y, at_z, core)

    place = (here, y, z)
    theirs, ours = 1 - x_lo, x_lo
    x_partner = device(x_hi, 1 - x_lo, y, z, core)
    other_core = device(x_hi, x_lo, y, z, 1 - core)

    barrier = pltpu.get_barrier_semaphore()

    def greet(target):
        pl.semaphore_signal(barrier, inc=1, device_id=target, device_id_type=MESH)

    for step in range(1, RING):
        greet(here(turn(y, step), z))
        greet(here(y, turn(z, step)))
    greet(x_partner)
    greet(other_core)

    @pl.when(core == 0)
    def _():
        for step in range(RING):
            greet(device(x_hi, x_lo, z, step, 1))

    @pl.when(core == 1)
    def _():
        greet(device(x_hi, 1 - x_lo, y, z, 0))

    @pl.when(x_hi == 1)
    def _():
        greet(device(0, x_lo, y, z, 1))

    expected = 8 + jnp.where(core == 0, 1, 4 + jnp.where(x_hi == 0, 2, 0))
    pl.semaphore_wait(barrier, expected)

    def product(lhs, rhs):
        return lax.dot_general(lhs[...], rhs[...], (((0,), (0,)), ((), ())), preferred_element_type=jnp.float32)

    def x_copy(which, half, at=None, target=None):
        at = which if at is None else at
        target = x_partner if target is None else target
        return remote(
            sent.at[which, half], got.at[at, half], x_send.at[which, half], x_recv.at[at, half], target
        )

    def last_copy(half):
        return x_copy(1, half, 2, device(x_hi, 1 - x_lo, y, z, 1))

    def partner_part(which, lhs, rhs, half):
        sent[which, half] = product(lhs.at[theirs], rhs.at[half])
        x_copy(which, half).start()

    def own_part(which, lhs, rhs, half):
        kept[which, half] = product(lhs.at[ours], rhs.at[half])

    def own_chunk(which, lhs, rhs, half, row_z, first):
        rows = pl.ds(pl.multiple_of(row_z * RING * ROWS, ROWS), RING * ROWS)
        value = product(lhs.at[0, rows], rhs.at[half, rows])
        kept[which, half] = value if first else kept[which, half] + value

    def out_copy(which, out, turned, half, owner, start):
        block, row_z = (z, y) if turned else (y, z)
        src = rounded.at[which, half, pl.ds(owner * OWNED, OWNED)]
        dst = out.at[:, pl.ds(pl.multiple_of(block * BLOCK + half * HALF, HALF), HALF)]
        if turned:
            recv = out_recv.at[1, block, half]
            copy = remote(src, dst, out_send.at[which, half, owner], recv, device(x_hi, x_lo, owner, row_z, 0))
            if start:
                copy.start()
            else:
                copy.wait_send()
            return
        recv = out_recv.at[which, block, half]

        @pl.when(owner == y)
        def _():
            if start:
                pltpu.make_async_copy(src, dst, recv).start()

        @pl.when(owner != y)
        def _():
            copy = remote(src, dst, out_send.at[which, half, owner], recv, here(owner, row_z))
            if start:
                copy.start()
            else:
                copy.wait_send()

    def finish(which, out, turned, half):
        x_copy(which, half).wait_recv() if which < 2 else x_copy(1, half, 2).wait_recv()
        rounded[which, half] = ((kept[which, half] + got[which, half]) * inverse).astype(jnp.bfloat16)
        for owner in range(RING):
            out_copy(which, out, turned, half, owner, True)

    def drain_sends(which, out, turned):
        @pl.loop(0, 2)
        def _(half):
            for owner in range(RING):
                out_copy(which, out, turned, half, owner, False)

    def drain_x(which):
        @pl.loop(0, 2)
        def _(half):
            x_copy(which, half).wait_send()

    def drain_out(which, out):
        @pl.loop(0, 2)
        def _(half):
            for block in range(RING):
                dst = out.at[:, pl.ds(pl.multiple_of(block * BLOCK + half * HALF, HALF), HALF)]
                remote(
                    rounded.at[which, half, pl.ds(0, OWNED)], dst, out_send.at[which, half, 0],
                    out_recv.at[which, block, half], x_partner,
                ).wait_recv()

    def spread_last(lasts):
        @pl.when(x_hi == 0)
        def _():
            lasts.spread(e_ref, 0)

        lasts.copies[0].clear()

        @pl.when(x_hi == 1)
        def _():
            for to in range(RING):
                relayed(core, to).wait_recv()
            lasts.spread(staged, 0)

        lasts.copies[0][:] = [None] * len(lasts.copies[0])

    def drain_last(lasts):
        whole = lasts.piece(0, lasts.mine)
        for count in range(RING - 1):
            remote(whole, whole, last_send.at[0, count], last_recv.at[0, 0], x_partner).wait_send()

    def relayed(to_core, to):
        half = lax.rem(to_core + theirs, 2)
        columns = pl.ds(pl.multiple_of(to * BLOCK + half * HALF, HALF), HALF)
        return remote(
            x_ref.at[:, columns], staged.at[:, columns], relay_send.at[to_core, to], relay_recv.at[to],
            device(1, x_lo, y, z, to_core),
        )

    @pl.when(core == 0)
    def _():
        lefts = Flow(place, left, left_send, left_recv, False, (theirs, ours))
        rights = Flow(place, right, right_send, right_recv, True, (0, 1))
        lasts = Flow(place, last, last_send, last_recv, True, (theirs,), (0,))
        passed = []

        def hand_over(order, index):
            half = lefts.halves[order]
            whole = lefts.piece(order, index)
            to = prev.at[half, pl.ds(pl.multiple_of(index * ROWS, ROWS), ROWS)]
            copy = remote(whole, to, pass_send.at[half, index], prev_recv.at[half, index], other_core)
            copy.start()
            passed.append(copy)

        def rest_left(order):
            for index in lefts.rest():
                lefts.wait(order, index)
                hand_over(order, index)

        def left_own(order, part):
            hand_over(order, lefts.own(order, part))

        def left_relay(order, step, part):
            hand_over(order, lefts.relay(order, step, part))

        lefts.spread(x_ref, 0)
        for part in PIECES:
            left_own(0, part)
        rights.spread(x_ref, 0)
        weave(left_relay, 0, rights.own, 0)
        lefts.spread(x_ref, 1)
        rest_left(0)
        weave(rights.relay, 0, left_own, 1)
        spread_last(lasts)
        rights.wait_rest(0)
        partner_part(0, left, right, 0)
        weave(left_relay, 1, lasts.own, 0)
        rights.spread(x_ref, 1)
        rest_left(1)
        weave(lasts.relay, 0, rights.own, 1)
        own_part(0, left, right, 0)
        lasts.wait_rest(0)
        for half in range(2):
            sent[1, half] = product(last.at[0], left.at[half])
            last_copy(half).start()
        for step, part in FORWARD:
            rights.relay(1, step, part)
        finish(0, d_ref, False, 0)
        rights.wait_rest(1)
        partner_part(0, left, right, 1)
        own_part(0, left, right, 1)
        finish(0, d_ref, False, 1)
        drain_x(0)
        drain_sends(0, d_ref, False)
        lefts.drain(0)
        lefts.drain(1)
        rights.drain(0)
        rights.drain(1)
        lasts.drain(0)
        drain_last(lasts)
        for copy in passed:
            copy.wait_send()
        for half in range(2):
            last_copy(half).wait_send()
        drain_out(0, d_ref)
        drain_out(1, a_ref)

    @pl.when(core == 1)
    def _():
        lefts = Flow(place, left, left_send, left_recv, False, (theirs, ours))
        rights = Flow(place, right, right_send, right_recv, True, (0, 1))
        prevs = Flow(place, prev, left_send, prev_recv, False, (theirs, ours))
        lasts = Flow(place, last, last_send, last_recv, True, (ours,), (0,))

        def wait_prev(order):
            for part in PIECES:
                prevs.wait(order, prevs.index(0, part))
            for step, part in FORWARD:
                prevs.wait(order, prevs.index(step, part))
            prevs.wait_rest(order)

        def relay_last(to_core):
            @pl.when(x_hi == 0)
            def _():
                for to in range(RING):
                    relayed(to_core, to).start()

        rights.spread(x_ref, 0)
        relay_last(0)
        relay_last(1)
        for part in PIECES:
            rights.own(0, part)
        lefts.spread(x_ref, 0)
        weave(rights.relay, 0, lefts.own, 0)
        rights.spread(x_ref, 1)
        rights.wait_rest(0)
        wait_prev(0)
        partner_part(1, prev, right, 0)
        weave(lefts.relay, 0, rights.own, 1)
        lefts.spread(x_ref, 1)
        lefts.wait_rest(0)
        partner_part(0, left, right, 0)
        weave(rights.relay, 1, lefts.own, 1)
        rights.wait_rest(1)
        partner_part(1, prev, right, 1)
        partner_part(0, left, right, 1)
        for step, part in FORWARD:
            lefts.relay(1, step, part)
        spread_last(lasts)
        wait_prev(1)
        own_part(1, prev, right, 0)
        own_part(1, prev, right, 1)
        for part in PIECES:
            lasts.own(0, part)
        finish(1, a_ref, False, 0)
        finish(1, a_ref, False, 1)
        for step, part in FORWARD[:2]:
            lasts.relay(0, step, part)
        lefts.wait_rest(1)
        own_part(0, left, right, 0)
        for step, part in FORWARD[2:]:
            lasts.relay(0, step, part)
        own_part(0, left, right, 1)
        for half in range(2):
            own_chunk(2, last, prev, half, z, True)
        finish(0, d_ref, False, 0)
        for step, part in lasts.REST[:4]:
            lasts.wait(0, lasts.index(step, part))
        for half in range(2):
            own_chunk(2, last, prev, half, turn(z, 1), False)
            own_chunk(2, last, prev, half, turn(z, -1), False)
        finish(0, d_ref, False, 1)
        for step, part in lasts.REST[4:]:
            lasts.wait(0, lasts.index(step, part))
        for half in range(2):
            own_chunk(2, last, prev, half, turn(z, 2), False)
            finish(2, a_ref, True, half)
        drain_x(0)
        drain_x(1)
        drain_sends(0, d_ref, False)
        drain_sends(1, a_ref, False)
        drain_sends(2, a_ref, True)
        for order in range(2):
            lefts.drain(order)
            rights.drain(order)
        lasts.drain(0)
        drain_last(lasts)

        @pl.when(x_hi == 0)
        def _():
            for to_core in range(2):
                for to in range(RING):
                    relayed(to_core, to).wait_send()

        drain_out(1, a_ref)
        drain_out(0, d_ref)


def on_device(factor_rows, entry_rows):
    rows, width = factor_rows.shape[2:]
    tokens = rows * lax.axis_size("dp")
    out = jax.ShapeDtypeStruct((OWNED, width), jnp.bfloat16)
    block = pltpu.VMEM((2, tokens // 2, HALF), jnp.bfloat16)
    part = pltpu.VMEM((3, 2, HALF, HALF), jnp.float32)
    slots = pltpu.SemaphoreType.DMA((2, 16))
    diagonal, adjacent = pl.pallas_call(
        functools.partial(kernel, 1.0 / tokens),
        out_shape=(out, out),
        in_specs=[pl.BlockSpec(memory_space=pl.ANY)] * 2,
        out_specs=[pl.BlockSpec(memory_space=pl.ANY)] * 2,
        scratch_shapes=[
            block, block, block, pltpu.VMEM((1, tokens // 2, HALF), jnp.bfloat16),
            pltpu.VMEM((rows, width), jnp.bfloat16),
            pltpu.VMEM((2, 2, HALF, HALF), jnp.float32), part, part, pltpu.VMEM((3, 2, HALF, HALF), jnp.bfloat16),
        ]
        + [slots] * 8
        + [
            pltpu.SemaphoreType.DMA((2, RING)),
            pltpu.SemaphoreType.DMA((RING,)),
            pltpu.SemaphoreType.DMA((2, 2)),
            pltpu.SemaphoreType.DMA((3, 2)),
            pltpu.SemaphoreType.DMA((3, 2, RING)),
            pltpu.SemaphoreType.DMA((2, RING, 2)),
        ],
        compiler_params=pltpu.CompilerParams(
            collective_id=0, has_side_effects=True, vmem_limit_bytes=60 * 2**20
        ),
        cost_estimate=pl.CostEstimate(flops=4 * BLOCK * BLOCK * tokens // 2, bytes_accessed=2**22, transcendentals=0),
        name="blocks",
    )(factor_rows.reshape(rows, width), entry_rows.reshape(rows, width))
    return diagonal.reshape(1, 1, OWNED, width), adjacent.reshape(1, 1, OWNED, width)


def solution(mesh):
    placed = (P(None, "section", "dp", None), P(None, "dp", None))
    return jax.shard_map(
        on_device,
        mesh=mesh,
        in_specs=placed,
        out_specs=(P(None, "section", "dp", None), P(None, "section", "dp", None)),
        check_vma=False,
    )
```

```python
import functools

import jax
import jax.numpy as jnp
from jax import lax
from jax.experimental import pallas as pl
from jax.experimental.pallas import tpu as pltpu
from jax.sharding import PartitionSpec as P

MESH = pl.DeviceIdType.MESH
RING = 4
ROWS = 192
BLOCK = 768
HALF = 384
OWNED = 96
DEPTH = 3
PIECES = (0, 1, 3, 2)
FORWARD = ((-1, 0), (1, 3), (-1, 1), (1, 2))


def device(x_hi, x_lo, y, z, core):
    return (x_hi * 2 + core, z * 8 + x_lo * 4 + y)


def turn(position, by):
    return lax.rem(position + by + RING, RING)


def remote(src, dst, send, recv, target):
    return pltpu.make_async_remote_copy(
        src_ref=src, dst_ref=dst, send_sem=send, recv_sem=recv, device_id=target, device_id_type=MESH
    )


def slot(row_z, row_y):
    return row_z * RING + row_y


class Flow:
    def __init__(self, place, buffer, send, recv, along_z, halves, kept=None):
        self.here, self.y, self.z = place
        self.buffer, self.send, self.recv, self.along_z, self.halves = buffer, send, recv, along_z, halves
        self.kept = halves if kept is None else kept
        self.copies = ([], [])
        self.flying = {1: [], -1: []}
        self.mine = slot(self.z, self.y)

    def piece(self, order, index):
        return self.buffer.at[self.kept[order], pl.ds(pl.multiple_of(index * ROWS, ROWS), ROWS)]

    def columns(self, src, order, block):
        start = pl.multiple_of(block * BLOCK + self.halves[order] * HALF, HALF)
        return src.at[:, pl.ds(start, HALF)]

    def start(self, src, order, index, target):
        half = self.kept[order]
        count = len(self.copies[order])
        copy = remote(src, self.piece(order, index), self.send.at[half, count], self.recv.at[half, index], target)
        copy.start()
        self.copies[order].append(copy)

    def wait(self, order, index):
        whole = self.piece(order, index)
        half = self.kept[order]
        remote(whole, whole, self.send.at[half, 0], self.recv.at[half, index], self.neighbour(1)).wait_recv()

    def spread(self, src, order):
        own = self.y if self.along_z else self.z
        pltpu.make_async_copy(
            self.columns(src, order, own), self.piece(order, self.mine), self.recv.at[self.kept[order], self.mine]
        ).start()
        for step in (1, 3, 2):
            to = turn(own, step)
            target = self.here(to, self.z) if self.along_z else self.here(self.y, to)
            self.start(self.columns(src, order, to), order, self.mine, target)

    def index(self, step, part):
        if self.along_z:
            return slot(turn(self.z, step), turn(self.y, part))
        return slot(turn(self.z, part), turn(self.y, step))

    def neighbour(self, step):
        return self.here(self.y, turn(self.z, step)) if self.along_z else self.here(turn(self.y, step), self.z)

    def push(self, order, index, step):
        flying = self.flying[step]
        if len(flying) == DEPTH:
            past, count = flying.pop(0)
            self.copies[past][count].wait_send()
            self.copies[past][count] = None
        flying.append((order, len(self.copies[order])))
        self.start(self.piece(order, index), order, index, self.neighbour(step))

    def own(self, order, part):
        index = self.index(0, part)
        self.wait(order, index)
        self.push(order, index, 1)
        self.push(order, index, -1)
        return index

    def relay(self, order, step, part):
        index = self.index(step, part)
        self.wait(order, index)
        self.push(order, index, -step)
        return index

    REST = ((-1, 3), (-1, 2), (1, 0), (1, 1), (2, 0), (2, 1), (2, 3), (2, 2))

    def rest(self):
        return [self.index(step, part) for step, part in self.REST]

    def wait_rest(self, order):
        for index in self.rest():
            self.wait(order, index)

    def drain(self, order, first=0):
        for copy in self.copies[order][first:]:
            if copy is not None:
                copy.wait_send()


def weave(relay, behind, own, ahead):
    relay(behind, *FORWARD[0])
    relay(behind, *FORWARD[1])
    own(ahead, 0)
    own(ahead, 1)
    relay(behind, *FORWARD[2])
    relay(behind, *FORWARD[3])
    own(ahead, 3)
    own(ahead, 2)


def kernel(
    inverse, x_ref, e_ref, d_ref, a_ref, left, right, prev, last, staged, sent, got, kept, rounded,
    left_send, left_recv, right_send, right_recv, prev_recv, last_send, last_recv, pass_send, relay_send, relay_recv,
    x_send, x_recv, out_send, out_recv,
):
    section = lax.axis_index("section")
    group = lax.axis_index("dp")
    x_hi, core = section // 2, lax.rem(section, 2)
    z, x_lo, y = group // 8, lax.rem(group // 4, 2), lax.rem(group, 4)

    def here(at_y, at_z):
        return device(x_hi, x_lo, at_y, at_z, core)

    place = (here, y, z)
    theirs, ours = 1 - x_lo, x_lo
    x_partner = device(x_hi, 1 - x_lo, y, z, core)
    other_core = device(x_hi, x_lo, y, z, 1 - core)

    barrier = pltpu.get_barrier_semaphore()

    def greet(target):
        pl.semaphore_signal(barrier, inc=1, device_id=target, device_id_type=MESH)

    for step in range(1, RING):
        greet(here(turn(y, step), z))
        greet(here(y, turn(z, step)))
    greet(x_partner)
    greet(other_core)

    @pl.when(core == 0)
    def _():
        for step in range(RING):
            greet(device(x_hi, x_lo, z, step, 1))

    @pl.when(core == 1)
    def _():
        greet(device(x_hi, 1 - x_lo, y, z, 0))

    @pl.when(x_hi == 1)
    def _():
        greet(device(0, x_lo, y, z, 1))

    expected = 8 + jnp.where(core == 0, 1, 4 + jnp.where(x_hi == 0, 2, 0))
    pl.semaphore_wait(barrier, expected)

    def product(lhs, rhs):
        return lax.dot_general(lhs[...], rhs[...], (((0,), (0,)), ((), ())), preferred_element_type=jnp.float32)

    class Pair:
        def __init__(self, *copies):
            self.copies = copies

        def start(self):
            for copy in self.copies:
                copy.start()

        def wait_send(self):
            for copy in self.copies:
                copy.wait_send()

    def x_copy(which, half, at=None, target=None):
        at = which if at is None else at
        target = x_partner if target is None else target
        halves = [pl.ds(0, HALF // 2), pl.ds(HALF // 2, HALF // 2)]
        return Pair(*(
            remote(
                sent.at[which, half, rows], got.at[at, half, rows],
                x_send.at[which, half, n], x_recv.at[at, half, n], target,
            )
            for n, rows in enumerate(halves)
        ))

    def last_copy(half):
        return x_copy(1, half, 2, device(x_hi, 1 - x_lo, y, z, 1))

    def partner_part(which, lhs, rhs, half):
        sent[which, half] = product(lhs.at[theirs], rhs.at[half])
        x_copy(which, half).start()

    def own_part(which, lhs, rhs, half):
        kept[which, half] = product(lhs.at[ours], rhs.at[half])

    def own_chunk(which, lhs, rhs, half, row_z, first):
        rows = pl.ds(pl.multiple_of(row_z * RING * ROWS, ROWS), RING * ROWS)
        value = product(lhs.at[0, rows], rhs.at[half, rows])
        kept[which, half] = value if first else kept[which, half] + value

    def out_copy(which, out, turned, half, owner, start):
        block, row_z = (z, y) if turned else (y, z)
        src = rounded.at[which, half, pl.ds(owner * OWNED, OWNED)]
        dst = out.at[:, pl.ds(pl.multiple_of(block * BLOCK + half * HALF, HALF), HALF)]
        if turned:
            recv = out_recv.at[1, block, half]
            copy = remote(src, dst, out_send.at[which, half, owner], recv, device(x_hi, x_lo, owner, row_z, 0))
            if start:
                copy.start()
            else:
                copy.wait_send()
            return
        recv = out_recv.at[which, block, half]

        @pl.when(owner == y)
        def _():
            if start:
                pltpu.make_async_copy(src, dst, recv).start()

        @pl.when(owner != y)
        def _():
            copy = remote(src, dst, out_send.at[which, half, owner], recv, here(owner, row_z))
            if start:
                copy.start()
            else:
                copy.wait_send()

    def finish(which, out, turned, half):
        arriving = x_copy(min(which, 1), half, which).copies
        for n in range(2):
            arriving[n].wait_recv()
            rows = pl.ds(n * HALF // 2, HALF // 2)
            total = kept[which, half, rows] + got[which, half, rows]
            rounded[which, half, rows] = (total * inverse).astype(jnp.bfloat16)
            for owner in (2 * n, 2 * n + 1):
                out_copy(which, out, turned, half, owner, True)

    def drain_sends(which, out, turned):
        @pl.loop(0, 2)
        def _(half):
            for owner in range(RING):
                out_copy(which, out, turned, half, owner, False)

    def drain_x(which):
        @pl.loop(0, 2)
        def _(half):
            x_copy(which, half).wait_send()

    def drain_out(which, out):
        @pl.loop(0, 2)
        def _(half):
            for block in range(RING):
                dst = out.at[:, pl.ds(pl.multiple_of(block * BLOCK + half * HALF, HALF), HALF)]
                remote(
                    rounded.at[which, half, pl.ds(0, OWNED)], dst, out_send.at[which, half, 0],
                    out_recv.at[which, block, half], x_partner,
                ).wait_recv()

    def spread_last(lasts):
        @pl.when(x_hi == 0)
        def _():
            lasts.spread(e_ref, 0)

        lasts.copies[0].clear()

        @pl.when(x_hi == 1)
        def _():
            for to in range(RING):
                relayed(core, to).wait_recv()
            lasts.spread(staged, 0)

        lasts.copies[0][:] = [None] * len(lasts.copies[0])

    def drain_last(lasts):
        whole = lasts.piece(0, lasts.mine)
        for count in range(RING - 1):
            remote(whole, whole, last_send.at[0, count], last_recv.at[0, 0], x_partner).wait_send()

    def relayed(to_core, to):
        half = lax.rem(to_core + theirs, 2)
        columns = pl.ds(pl.multiple_of(to * BLOCK + half * HALF, HALF), HALF)
        return remote(
            x_ref.at[:, columns], staged.at[:, columns], relay_send.at[to_core, to], relay_recv.at[to],
            device(1, x_lo, y, z, to_core),
        )

    @pl.when(core == 0)
    def _():
        lefts = Flow(place, left, left_send, left_recv, False, (theirs, ours))
        rights = Flow(place, right, right_send, right_recv, True, (0, 1))
        lasts = Flow(place, last, last_send, last_recv, True, (theirs,), (0,))
        passed = []

        def hand_over(order, index):
            half = lefts.halves[order]
            whole = lefts.piece(order, index)
            to = prev.at[half, pl.ds(pl.multiple_of(index * ROWS, ROWS), ROWS)]
            copy = remote(whole, to, pass_send.at[half, index], prev_recv.at[half, index], other_core)
            copy.start()
            passed.append(copy)

        def rest_left(order):
            for index in lefts.rest():
                lefts.wait(order, index)
                hand_over(order, index)

        def left_own(order, part):
            hand_over(order, lefts.own(order, part))

        def left_relay(order, step, part):
            hand_over(order, lefts.relay(order, step, part))

        lefts.spread(x_ref, 0)
        for part in PIECES:
            left_own(0, part)
        rights.spread(x_ref, 0)
        weave(left_relay, 0, rights.own, 0)
        lefts.spread(x_ref, 1)
        rest_left(0)
        weave(rights.relay, 0, left_own, 1)
        spread_last(lasts)
        rights.wait_rest(0)
        partner_part(0, left, right, 0)
        weave(left_relay, 1, lasts.own, 0)
        rights.spread(x_ref, 1)
        rest_left(1)
        weave(lasts.relay, 0, rights.own, 1)
        rights.relay(1, -1, 0)
        lasts.wait_rest(0)
        rights.relay(1, -1, 1)
        for half in range(2):
            sent[1, half] = product(last.at[0], left.at[half])
            last_copy(half).start()
            rights.relay(1, 1, 3 - half)
        own_part(0, left, right, 0)
        lefts.drain(0)
        lefts.drain(1)
        rights.drain(0)
        for copy in passed:
            copy.wait_send()
        rights.wait_rest(1)
        partner_part(0, left, right, 1)
        finish(0, d_ref, False, 0)
        own_part(0, left, right, 1)
        finish(0, d_ref, False, 1)
        rights.drain(1)
        lasts.drain(0)
        drain_last(lasts)
        drain_x(0)
        drain_sends(0, d_ref, False)
        for half in range(2):
            last_copy(half).wait_send()
        drain_out(0, d_ref)
        drain_out(1, a_ref)

    @pl.when(core == 1)
    def _():
        lefts = Flow(place, left, left_send, left_recv, False, (theirs, ours))
        rights = Flow(place, right, right_send, right_recv, True, (0, 1))
        prevs = Flow(place, prev, left_send, prev_recv, False, (theirs, ours))
        lasts = Flow(place, last, last_send, last_recv, True, (ours,), (0,))

        def wait_prev(order):
            for part in PIECES:
                prevs.wait(order, prevs.index(0, part))
            for step, part in FORWARD:
                prevs.wait(order, prevs.index(step, part))
            prevs.wait_rest(order)

        def relay_last(to_core):
            @pl.when(x_hi == 0)
            def _():
                for to in range(RING):
                    relayed(to_core, to).start()

        rights.spread(x_ref, 0)
        relay_last(0)
        relay_last(1)
        for part in PIECES:
            rights.own(0, part)
        lefts.spread(x_ref, 0)
        weave(rights.relay, 0, lefts.own, 0)
        rights.spread(x_ref, 1)
        rights.wait_rest(0)
        wait_prev(0)
        partner_part(1, prev, right, 0)
        weave(lefts.relay, 0, rights.own, 1)
        lefts.spread(x_ref, 1)
        lefts.wait_rest(0)
        partner_part(0, left, right, 0)
        weave(rights.relay, 1, lefts.own, 1)
        rights.wait_rest(1)
        partner_part(1, prev, right, 1)
        partner_part(0, left, right, 1)
        for step, part in FORWARD:
            lefts.relay(1, step, part)
        spread_last(lasts)
        wait_prev(1)
        own_part(1, prev, right, 0)
        own_part(1, prev, right, 1)
        for part in PIECES:
            lasts.own(0, part)
        finish(1, a_ref, False, 0)
        finish(1, a_ref, False, 1)
        for step, part in FORWARD[:2]:
            lasts.relay(0, step, part)
        lefts.wait_rest(1)
        own_part(0, left, right, 0)
        for step, part in FORWARD[2:]:
            lasts.relay(0, step, part)
        own_part(0, left, right, 1)
        for half in range(2):
            own_chunk(2, last, prev, half, z, True)
        finish(0, d_ref, False, 0)
        for step, part in lasts.REST[:4]:
            lasts.wait(0, lasts.index(step, part))
        for half in range(2):
            own_chunk(2, last, prev, half, turn(z, 1), False)
            own_chunk(2, last, prev, half, turn(z, -1), False)
        finish(0, d_ref, False, 1)
        for order in range(2):
            lefts.drain(order)
            rights.drain(order)

        @pl.when(x_hi == 0)
        def _():
            for to_core in range(2):
                for to in range(RING):
                    relayed(to_core, to).wait_send()

        drain_x(0)
        drain_x(1)
        drain_sends(0, d_ref, False)
        drain_sends(1, a_ref, False)
        for step, part in lasts.REST[4:]:
            lasts.wait(0, lasts.index(step, part))
        for half in range(2):
            own_chunk(2, last, prev, half, turn(z, 2), False)
            finish(2, a_ref, True, half)
        lasts.drain(0)
        drain_last(lasts)
        drain_sends(2, a_ref, True)
        drain_out(1, a_ref)
        drain_out(0, d_ref)


def copies(first, second, first_out, second_out):
    first_out[...] = first[...]
    second_out[...] = second[...]


def on_device(factor_rows, entry_rows):
    rows, width = factor_rows.shape[2:]
    tokens = rows * lax.axis_size("dp")
    out = jax.ShapeDtypeStruct((OWNED, width), jnp.bfloat16)
    block = pltpu.VMEM((2, tokens // 2, HALF), jnp.bfloat16)
    part = pltpu.VMEM((3, 2, HALF, HALF), jnp.float32)
    slots = pltpu.SemaphoreType.DMA((2, 16))
    diagonal, adjacent = pl.pallas_call(
        functools.partial(kernel, 1.0 / tokens),
        out_shape=(out, out),
        in_specs=[pl.BlockSpec(memory_space=pl.ANY)] * 2,
        out_specs=[pl.BlockSpec(memory_space=pl.ANY)] * 2,
        scratch_shapes=[
            block, block, block, pltpu.VMEM((1, tokens // 2, HALF), jnp.bfloat16),
            pltpu.VMEM((rows, width), jnp.bfloat16),
            pltpu.VMEM((2, 2, HALF, HALF), jnp.float32), part, part, pltpu.VMEM((3, 2, HALF, HALF), jnp.bfloat16),
        ]
        + [slots] * 8
        + [
            pltpu.SemaphoreType.DMA((2, RING)),
            pltpu.SemaphoreType.DMA((RING,)),
            pltpu.SemaphoreType.DMA((2, 2, 2)),
            pltpu.SemaphoreType.DMA((3, 2, 2)),
            pltpu.SemaphoreType.DMA((3, 2, RING)),
            pltpu.SemaphoreType.DMA((2, RING, 2)),
        ],
        compiler_params=pltpu.CompilerParams(
            collective_id=0, has_side_effects=True, vmem_limit_bytes=60 * 2**20
        ),
        cost_estimate=pl.CostEstimate(flops=4 * BLOCK * BLOCK * tokens // 2, bytes_accessed=2**22, transcendentals=0),
        name="blocks",
    )(factor_rows.reshape(rows, width), entry_rows.reshape(rows, width))
    diagonal, adjacent = pl.pallas_call(copies, out_shape=(out, out), name="outputs")(diagonal, adjacent)
    return diagonal.reshape(1, 1, OWNED, width), adjacent.reshape(1, 1, OWNED, width)


def solution(mesh):
    placed = (P(None, "section", "dp", None), P(None, "dp", None))
    return jax.shard_map(
        on_device,
        mesh=mesh,
        in_specs=placed,
        out_specs=(P(None, "section", "dp", None), P(None, "section", "dp", None)),
        check_vma=False,
    )
```

```python
import functools

import jax
import jax.numpy as jnp
from jax import lax
from jax.experimental import pallas as pl
from jax.experimental.pallas import tpu as pltpu
from jax.sharding import PartitionSpec as P

MESH = pl.DeviceIdType.MESH
RING = 4
ROWS = 192
BLOCK = 768
HALF = 384
OWNED = 96
DEPTH = 16
PIECES = (0, 1, 3, 2)
FORWARD = ((-1, 0), (1, 3), (-1, 1), (1, 2))


def device(x_hi, x_lo, y, z, core):
    return (x_hi * 2 + core, z * 8 + x_lo * 4 + y)


def turn(position, by):
    return lax.rem(position + by + RING, RING)


def remote(src, dst, send, recv, target):
    return pltpu.make_async_remote_copy(
        src_ref=src, dst_ref=dst, send_sem=send, recv_sem=recv, device_id=target, device_id_type=MESH
    )


def slot(row_z, row_y):
    return row_z * RING + row_y


class Flow:
    def __init__(self, place, buffer, send, recv, along_z, halves, kept=None):
        self.here, self.y, self.z = place
        self.buffer, self.send, self.recv, self.along_z, self.halves = buffer, send, recv, along_z, halves
        self.kept = halves if kept is None else kept
        self.copies = ([], [])
        self.flying = {1: [], -1: []}
        self.mine = slot(self.z, self.y)

    def piece(self, order, index):
        return self.buffer.at[self.kept[order], pl.ds(pl.multiple_of(index * ROWS, ROWS), ROWS)]

    def columns(self, src, order, block):
        start = pl.multiple_of(block * BLOCK + self.halves[order] * HALF, HALF)
        return src.at[:, pl.ds(start, HALF)]

    def start(self, src, order, index, target):
        half = self.kept[order]
        count = len(self.copies[order])
        copy = remote(src, self.piece(order, index), self.send.at[half, count], self.recv.at[half, index], target)
        copy.start()
        self.copies[order].append(copy)

    def wait(self, order, index):
        whole = self.piece(order, index)
        half = self.kept[order]
        remote(whole, whole, self.send.at[half, 0], self.recv.at[half, index], self.neighbour(1)).wait_recv()

    def spread(self, src, order):
        own = self.y if self.along_z else self.z
        pltpu.make_async_copy(
            self.columns(src, order, own), self.piece(order, self.mine), self.recv.at[self.kept[order], self.mine]
        ).start()
        for step in (1, 3, 2):
            to = turn(own, step)
            target = self.here(to, self.z) if self.along_z else self.here(self.y, to)
            self.start(self.columns(src, order, to), order, self.mine, target)

    def index(self, step, part):
        if self.along_z:
            return slot(turn(self.z, step), turn(self.y, part))
        return slot(turn(self.z, part), turn(self.y, step))

    def neighbour(self, step):
        return self.here(self.y, turn(self.z, step)) if self.along_z else self.here(turn(self.y, step), self.z)

    def push(self, order, index, step):
        flying = self.flying[step]
        if len(flying) == DEPTH:
            past, count = flying.pop(0)
            self.copies[past][count].wait_send()
            self.copies[past][count] = None
        flying.append((order, len(self.copies[order])))
        self.start(self.piece(order, index), order, index, self.neighbour(step))

    def own(self, order, part):
        index = self.index(0, part)
        self.wait(order, index)
        self.push(order, index, 1)
        self.push(order, index, -1)
        return index

    def relay(self, order, step, part):
        index = self.index(step, part)
        self.wait(order, index)
        self.push(order, index, -step)
        return index

    REST = ((-1, 3), (-1, 2), (1, 0), (1, 1), (2, 0), (2, 1), (2, 3), (2, 2))

    def rest(self):
        return [self.index(step, part) for step, part in self.REST]

    def wait_rest(self, order):
        for index in self.rest():
            self.wait(order, index)

    def drain(self, order, first=0):
        for copy in self.copies[order][first:]:
            if copy is not None:
                copy.wait_send()


def weave(relay, behind, own, ahead):
    relay(behind, *FORWARD[0])
    relay(behind, *FORWARD[1])
    relay(behind, *FORWARD[2])
    relay(behind, *FORWARD[3])
    own(ahead, 0)
    own(ahead, 1)
    own(ahead, 3)
    own(ahead, 2)


def kernel(
    inverse, x_ref, e_ref, d_ref, a_ref, left, right, prev, last, staged, sent, got, kept, rounded,
    left_send, left_recv, right_send, right_recv, prev_recv, last_send, last_recv, pass_send, relay_send, relay_recv,
    x_send, x_recv, out_send, out_recv,
):
    section = lax.axis_index("section")
    group = lax.axis_index("dp")
    x_hi, core = section // 2, lax.rem(section, 2)
    z, x_lo, y = group // 8, lax.rem(group // 4, 2), lax.rem(group, 4)

    def here(at_y, at_z):
        return device(x_hi, x_lo, at_y, at_z, core)

    place = (here, y, z)
    theirs, ours = 1 - x_lo, x_lo
    x_partner = device(x_hi, 1 - x_lo, y, z, core)
    other_core = device(x_hi, x_lo, y, z, 1 - core)

    barrier = pltpu.get_barrier_semaphore()

    def greet(target):
        pl.semaphore_signal(barrier, inc=1, device_id=target, device_id_type=MESH)

    for step in range(1, RING):
        greet(here(turn(y, step), z))
        greet(here(y, turn(z, step)))
    greet(x_partner)
    greet(other_core)

    @pl.when(core == 0)
    def _():
        for step in range(RING):
            greet(device(x_hi, x_lo, z, step, 1))

    @pl.when(core == 1)
    def _():
        greet(device(x_hi, 1 - x_lo, y, z, 0))

    @pl.when(x_hi == 1)
    def _():
        greet(device(0, x_lo, y, z, 1))

    expected = 8 + jnp.where(core == 0, 1, 4 + jnp.where(x_hi == 0, 2, 0))
    pl.semaphore_wait(barrier, expected)

    def product(lhs, rhs):
        return lax.dot_general(lhs[...], rhs[...], (((0,), (0,)), ((), ())), preferred_element_type=jnp.float32)

    class Pair:
        def __init__(self, *copies):
            self.copies = copies

        def start(self):
            for copy in self.copies:
                copy.start()

        def wait_send(self):
            for copy in self.copies:
                copy.wait_send()

    def x_copy(which, half, at=None, target=None):
        at = which if at is None else at
        target = x_partner if target is None else target
        halves = [pl.ds(0, HALF // 2), pl.ds(HALF // 2, HALF // 2)]
        return Pair(*(
            remote(
                sent.at[which, half, rows], got.at[at, half, rows],
                x_send.at[which, half, n], x_recv.at[at, half, n], target,
            )
            for n, rows in enumerate(halves)
        ))

    def last_copy(half):
        return x_copy(1, half, 2, device(x_hi, 1 - x_lo, y, z, 1))

    def partner_part(which, lhs, rhs, half):
        sent[which, half] = product(lhs.at[theirs], rhs.at[half])
        x_copy(which, half).start()

    def own_part(which, lhs, rhs, half):
        kept[which, half] = product(lhs.at[ours], rhs.at[half])

    def own_chunk(which, lhs, rhs, half, row_z, first):
        rows = pl.ds(pl.multiple_of(row_z * RING * ROWS, ROWS), RING * ROWS)
        value = product(lhs.at[0, rows], rhs.at[half, rows])
        kept[which, half] = value if first else kept[which, half] + value

    def out_copy(which, out, turned, half, owner, start):
        block, row_z = (z, y) if turned else (y, z)
        src = rounded.at[which, half, pl.ds(owner * OWNED, OWNED)]
        dst = out.at[:, pl.ds(pl.multiple_of(block * BLOCK + half * HALF, HALF), HALF)]
        if turned:
            recv = out_recv.at[1, block, half]
            copy = remote(src, dst, out_send.at[which, half, owner], recv, device(x_hi, x_lo, owner, row_z, 0))
            if start:
                copy.start()
            else:
                copy.wait_send()
            return
        recv = out_recv.at[which, block, half]

        @pl.when(owner == y)
        def _():
            if start:
                pltpu.make_async_copy(src, dst, recv).start()

        @pl.when(owner != y)
        def _():
            copy = remote(src, dst, out_send.at[which, half, owner], recv, here(owner, row_z))
            if start:
                copy.start()
            else:
                copy.wait_send()

    def finish(which, out, turned, half):
        arriving = x_copy(min(which, 1), half, which).copies
        for n in range(2):
            arriving[n].wait_recv()
            rows = pl.ds(n * HALF // 2, HALF // 2)
            total = kept[which, half, rows] + got[which, half, rows]
            rounded[which, half, rows] = (total * inverse).astype(jnp.bfloat16)
            for owner in (2 * n, 2 * n + 1):
                out_copy(which, out, turned, half, owner, True)

    def drain_sends(which, out, turned):
        @pl.loop(0, 2)
        def _(half):
            for owner in range(RING):
                out_copy(which, out, turned, half, owner, False)

    def drain_x(which):
        @pl.loop(0, 2)
        def _(half):
            x_copy(which, half).wait_send()

    def drain_out(which, out):
        @pl.loop(0, 2)
        def _(half):
            for block in range(RING):
                dst = out.at[:, pl.ds(pl.multiple_of(block * BLOCK + half * HALF, HALF), HALF)]
                remote(
                    rounded.at[which, half, pl.ds(0, OWNED)], dst, out_send.at[which, half, 0],
                    out_recv.at[which, block, half], x_partner,
                ).wait_recv()

    def spread_last(lasts):
        @pl.when(x_hi == 0)
        def _():
            lasts.spread(e_ref, 0)

        lasts.copies[0].clear()

        @pl.when(x_hi == 1)
        def _():
            for to in range(RING):
                relayed(core, to).wait_recv()
            lasts.spread(staged, 0)

        lasts.copies[0][:] = [None] * len(lasts.copies[0])

    def drain_last(lasts):
        whole = lasts.piece(0, lasts.mine)
        for count in range(RING - 1):
            remote(whole, whole, last_send.at[0, count], last_recv.at[0, 0], x_partner).wait_send()

    def relayed(to_core, to):
        half = lax.rem(to_core + theirs, 2)
        columns = pl.ds(pl.multiple_of(to * BLOCK + half * HALF, HALF), HALF)
        return remote(
            x_ref.at[:, columns], staged.at[:, columns], relay_send.at[to_core, to], relay_recv.at[to],
            device(1, x_lo, y, z, to_core),
        )

    @pl.when(core == 0)
    def _():
        lefts = Flow(place, left, left_send, left_recv, False, (theirs, ours))
        rights = Flow(place, right, right_send, right_recv, True, (0, 1))
        lasts = Flow(place, last, last_send, last_recv, True, (theirs,), (0,))
        passed = []

        def hand_over(order, index):
            half = lefts.halves[order]
            whole = lefts.piece(order, index)
            to = prev.at[half, pl.ds(pl.multiple_of(index * ROWS, ROWS), ROWS)]
            copy = remote(whole, to, pass_send.at[half, index], prev_recv.at[half, index], other_core)
            copy.start()
            passed.append(copy)

        def rest_left(order):
            for index in lefts.rest():
                lefts.wait(order, index)
                hand_over(order, index)

        def left_own(order, part):
            hand_over(order, lefts.own(order, part))

        def left_relay(order, step, part):
            hand_over(order, lefts.relay(order, step, part))

        lefts.spread(x_ref, 0)
        for part in PIECES:
            left_own(0, part)
        rights.spread(x_ref, 0)
        weave(left_relay, 0, rights.own, 0)
        lefts.spread(x_ref, 1)
        rest_left(0)
        weave(rights.relay, 0, left_own, 1)
        spread_last(lasts)
        rights.wait_rest(0)
        partner_part(0, left, right, 0)
        weave(left_relay, 1, lasts.own, 0)
        rights.spread(x_ref, 1)
        rest_left(1)
        weave(lasts.relay, 0, rights.own, 1)
        rights.relay(1, -1, 0)
        lasts.wait_rest(0)
        rights.relay(1, -1, 1)
        for half in range(2):
            sent[1, half] = product(last.at[0], left.at[half])
            last_copy(half).start()
            rights.relay(1, 1, 3 - half)
        own_part(0, left, right, 0)
        lefts.drain(0)
        lefts.drain(1)
        rights.drain(0)
        for copy in passed:
            copy.wait_send()
        rights.wait_rest(1)
        partner_part(0, left, right, 1)
        finish(0, d_ref, False, 0)
        own_part(0, left, right, 1)
        finish(0, d_ref, False, 1)
        rights.drain(1)
        lasts.drain(0)
        drain_last(lasts)
        drain_x(0)
        drain_sends(0, d_ref, False)
        for half in range(2):
            last_copy(half).wait_send()
        drain_out(0, d_ref)
        drain_out(1, a_ref)

    @pl.when(core == 1)
    def _():
        lefts = Flow(place, left, left_send, left_recv, False, (theirs, ours))
        rights = Flow(place, right, right_send, right_recv, True, (0, 1))
        prevs = Flow(place, prev, left_send, prev_recv, False, (theirs, ours))
        lasts = Flow(place, last, last_send, last_recv, True, (ours,), (0,))

        def wait_prev(order):
            for part in PIECES:
                prevs.wait(order, prevs.index(0, part))
            for step, part in FORWARD:
                prevs.wait(order, prevs.index(step, part))
            prevs.wait_rest(order)

        def relay_last(to_core):
            @pl.when(x_hi == 0)
            def _():
                for to in range(RING):
                    relayed(to_core, to).start()

        rights.spread(x_ref, 0)
        relay_last(0)
        relay_last(1)
        for part in PIECES:
            rights.own(0, part)
        lefts.spread(x_ref, 0)
        weave(rights.relay, 0, lefts.own, 0)
        rights.spread(x_ref, 1)
        rights.wait_rest(0)
        wait_prev(0)
        partner_part(1, prev, right, 0)
        weave(lefts.relay, 0, rights.own, 1)
        lefts.spread(x_ref, 1)
        lefts.wait_rest(0)
        partner_part(0, left, right, 0)
        weave(rights.relay, 1, lefts.own, 1)
        rights.wait_rest(1)
        partner_part(1, prev, right, 1)
        partner_part(0, left, right, 1)
        for step, part in FORWARD:
            lefts.relay(1, step, part)
        spread_last(lasts)
        wait_prev(1)
        own_part(1, prev, right, 0)
        own_part(1, prev, right, 1)
        for part in PIECES:
            lasts.own(0, part)
        finish(1, a_ref, False, 0)
        finish(1, a_ref, False, 1)
        for step, part in FORWARD[:2]:
            lasts.relay(0, step, part)
        lefts.wait_rest(1)
        own_part(0, left, right, 0)
        for step, part in FORWARD[2:]:
            lasts.relay(0, step, part)
        own_part(0, left, right, 1)
        for half in range(2):
            own_chunk(2, last, prev, half, z, True)
        finish(0, d_ref, False, 0)
        for step, part in lasts.REST[:4]:
            lasts.wait(0, lasts.index(step, part))
        for half in range(2):
            own_chunk(2, last, prev, half, turn(z, 1), False)
            own_chunk(2, last, prev, half, turn(z, -1), False)
        finish(0, d_ref, False, 1)
        for order in range(2):
            lefts.drain(order)
            rights.drain(order)

        @pl.when(x_hi == 0)
        def _():
            for to_core in range(2):
                for to in range(RING):
                    relayed(to_core, to).wait_send()

        drain_x(0)
        drain_x(1)
        drain_sends(0, d_ref, False)
        drain_sends(1, a_ref, False)
        for step, part in lasts.REST[4:]:
            lasts.wait(0, lasts.index(step, part))
        for half in range(2):
            own_chunk(2, last, prev, half, turn(z, 2), False)
            finish(2, a_ref, True, half)
        lasts.drain(0)
        drain_last(lasts)
        drain_sends(2, a_ref, True)
        drain_out(1, a_ref)
        drain_out(0, d_ref)


def copies(first, second, first_out, second_out):
    first_out[...] = first[...]
    second_out[...] = second[...]


def on_device(factor_rows, entry_rows):
    rows, width = factor_rows.shape[2:]
    tokens = rows * lax.axis_size("dp")
    out = jax.ShapeDtypeStruct((OWNED, width), jnp.bfloat16)
    block = pltpu.VMEM((2, tokens // 2, HALF), jnp.bfloat16)
    part = pltpu.VMEM((3, 2, HALF, HALF), jnp.float32)
    slots = pltpu.SemaphoreType.DMA((2, 16))
    diagonal, adjacent = pl.pallas_call(
        functools.partial(kernel, 1.0 / tokens),
        out_shape=(out, out),
        in_specs=[pl.BlockSpec(memory_space=pl.ANY)] * 2,
        out_specs=[pl.BlockSpec(memory_space=pl.ANY)] * 2,
        scratch_shapes=[
            block, block, block, pltpu.VMEM((1, tokens // 2, HALF), jnp.bfloat16),
            pltpu.VMEM((rows, width), jnp.bfloat16),
            pltpu.VMEM((2, 2, HALF, HALF), jnp.float32), part, part, pltpu.VMEM((3, 2, HALF, HALF), jnp.bfloat16),
        ]
        + [slots] * 8
        + [
            pltpu.SemaphoreType.DMA((2, RING)),
            pltpu.SemaphoreType.DMA((RING,)),
            pltpu.SemaphoreType.DMA((2, 2, 2)),
            pltpu.SemaphoreType.DMA((3, 2, 2)),
            pltpu.SemaphoreType.DMA((3, 2, RING)),
            pltpu.SemaphoreType.DMA((2, RING, 2)),
        ],
        compiler_params=pltpu.CompilerParams(
            collective_id=0, has_side_effects=True, vmem_limit_bytes=60 * 2**20
        ),
        cost_estimate=pl.CostEstimate(flops=4 * BLOCK * BLOCK * tokens // 2, bytes_accessed=2**22, transcendentals=0),
        name="blocks",
    )(factor_rows.reshape(rows, width), entry_rows.reshape(rows, width))
    diagonal, adjacent = pl.pallas_call(copies, out_shape=(out, out), name="outputs")(diagonal, adjacent)
    return diagonal.reshape(1, 1, OWNED, width), adjacent.reshape(1, 1, OWNED, width)


def solution(mesh):
    placed = (P(None, "section", "dp", None), P(None, "dp", None))
    return jax.shard_map(
        on_device,
        mesh=mesh,
        in_specs=placed,
        out_specs=(P(None, "section", "dp", None), P(None, "section", "dp", None)),
        check_vma=False,
    )
```
